256 devices in a mesh: wide: 32 (over y, z_hi, core), train: 8 (over x, z_lo).
Axes of the slice: x: 4, y: 4, z: 8 (z_hi: 4, z_lo: 2; z = z_hi * 2 + z_lo), core: 2. Of those that a mesh axis runs over, the one named last changes fastest.
Arguments:
- precond: bfloat16 [16384, 16384], P('wide', 'train'), may hold values from -0.1 to 2.1
- target_feats: bfloat16 [1536, 16384], P(None, 'train'), may hold values from -6 to 6
- train_feats: bfloat16 [8192, 16384], P('train', 'wide'), may hold values from -0.046875 to 0.046875
Outputs:
- scores: float32 [1536, 8192], P('wide', 'train')
The draws below stay inside these ranges and needn't reach their ends.
All inputs are finite; a program needn't handle non-finite values.
Results may differ from the reference program's by a relative error of at most 0.0029.
Values may be sent and summed in bfloat16 or wider, within the bound.
No kernel may reach another device: no remote copies, remote signals or barrier semaphores. Data moves between devices by JAX's collectives and lax.ppermute only.
A program may use at most 128 MiB of HBM per device.

```python
import math
import jax
import jax.numpy as jnp
from jax import lax

PROJ_DIM = 16384
TARGETS = 1536
TRAIN_ALL = 8192


def draw_precond(key, part):
    key = jax.random.fold_in(key, 7)
    noise_key, diag_key = jax.random.split(key)
    spread = 0.5 * jax.random.truncated_normal(noise_key, -3.0, 3.0, (PROJ_DIM, PROJ_DIM), jnp.float32)
    scale = jnp.exp(jax.random.uniform(diag_key, (PROJ_DIM,), jnp.float32, math.log(0.5), math.log(2.0)))
    row_ids = lax.broadcasted_iota(jnp.int32, (PROJ_DIM, PROJ_DIM), 0)
    col_ids = lax.broadcasted_iota(jnp.int32, (PROJ_DIM, PROJ_DIM), 1)
    full = spread / math.sqrt(PROJ_DIM) + jnp.where(row_ids == col_ids, scale[:, None], 0.0)
    return full.astype(jnp.bfloat16)


def block_scale(own_key, extent, pieces, least, high):
    level, own = 1.0, jax.random.fold_in(own_key, 6)
    for axis_at, parts in pieces:
        steps = jnp.exp(jax.random.uniform(jax.random.fold_in(own, axis_at), (parts,), jnp.float32, least / len(pieces), high / len(pieces)))
        level = level * jnp.repeat(steps, extent[axis_at] // parts).reshape([-1 if axis == axis_at else 1 for axis in range(len(extent))])
    return level


def scatter_about(rng, extent, scale, bound, cuts=(), kind=jnp.bfloat16):
    level = block_scale(rng, extent, cuts, -0.22, 0.18) if cuts else 1.0
    array = jax.random.normal(rng, extent, jnp.float32) * scale * level
    return jnp.minimum(jnp.maximum(array, -bound), bound).astype(kind)


def setup_inputs(seed: int = 0) -> dict:
    streams_of = jax.random.split(jax.random.key(seed), 4)
    precond = draw_precond(jax.random.fold_in(streams_of[3], 71), 0)
    target_feats = scatter_about(streams_of[1], (TARGETS, PROJ_DIM), 1.0, 6.0, ((1, 8),))
    train_feats = scatter_about(streams_of[2], (TRAIN_ALL, PROJ_DIM), PROJ_DIM ** -0.5, 0.046875, ((0, 8), (1, 32)))
    return {"precond": precond, "target_feats": target_feats, "train_feats": train_feats}


def reference(precond, target_feats, train_feats):
    panel = lax.dot_general(precond, target_feats, (((1,), (1,)), ((), ())), preferred_element_type=jnp.float32)
    panel_low = panel.astype(jnp.bfloat16)
    return lax.dot_general(panel_low, train_feats, (((0,), (1,)), ((), ())), preferred_element_type=jnp.float32)
```

```python
import jax
import jax.numpy as jnp
from jax import lax
from jax.sharding import PartitionSpec as P

Y, ZH, CORES = 4, 4, 2
BF16, F16, F32 = jnp.bfloat16, jnp.float16, jnp.float32
NT = (((1,), (1,)), ((), ()))


def wide_index(y, zh, c):
    return (y * ZH + zh) * CORES + c


def wide_shift(dy, dz, dc):
    return [
        (wide_index(y, z, c), wide_index((y + dy) % Y, (z + dz) % ZH, (c + dc) % CORES))
        for y in range(Y)
        for z in range(ZH)
        for c in range(CORES)
    ]


def shards(precond, target_feats, train_feats):
    w = lax.axis_index("wide")
    y, zh, c = w // (ZH * CORES), (w // CORES) % ZH, w % CORES
    feats = [train_feats] + [lax.ppermute(train_feats, "wide", wide_shift(s, 0, 0)) for s in range(1, Y)]
    part = lax.dot_general(target_feats, precond, NT, preferred_element_type=F32).astype(F16)
    part = part.reshape(Y, 8, 48, 512).transpose(1, 0, 2, 3)
    got = lax.all_to_all(part, "train", 0, 0)

    def owned(s):
        mine = lax.dynamic_index_in_dim(got, (y + s) % Y, 1, keepdims=False)
        return jnp.sum(mine.astype(F32), 0).astype(BF16)

    pieces = [owned(0)] + [lax.ppermute(owned(s), "wide", wide_shift(s, 0, 0)) for s in range(1, Y)]
    panel = jnp.stack(pieces)
    panel = lax.all_to_all(jnp.broadcast_to(panel[None], (8, Y, 48, 512)), "train", 0, 0)
    scores = sum(
        lax.dot_general(panel[:, s].reshape(384, 512), feats[s], NT, preferred_element_type=F32) for s in range(Y)
    ).reshape(ZH, CORES, 48, 1024)
    keep = lax.dynamic_index_in_dim(scores, c, 1, keepdims=False)
    send = lax.dynamic_index_in_dim(scores, 1 - c, 1, keepdims=False)
    both = keep + lax.ppermute(send, "wide", wide_shift(0, 0, 1))

    def block(s):
        return lax.dynamic_index_in_dim(both, (zh + s) % ZH, 0, keepdims=False)

    out = block(0)
    for s in range(1, ZH):
        out = out + lax.ppermute(block(s).astype(BF16), "wide", wide_shift(0, s, 0)).astype(F32)
    return out


def solution(mesh):
    in_specs = (P("wide", "train"), P(None, "train"), P("train", "wide"))
    out_specs = P("wide", "train")
    return jax.shard_map(shards, mesh=mesh, in_specs=in_specs, out_specs=out_specs, check_vma=False)
```

```python
import jax
import jax.numpy as jnp
from jax import lax
from jax.experimental import pallas as pl
from jax.experimental.pallas import tpu as pltpu
from jax.sharding import PartitionSpec as P

Y, ZH, CORES, X, ZL = 4, 4, 2, 4, 2
ROWS, DEPTH, TRAIN = 48, 512, 1024
COLS = 512
BF16, F16, F32 = jnp.bfloat16, jnp.float16, jnp.float32
NT = (((1,), (1,)), ((), ()))


def wide_shift(dy, dz, dc):
    def index(y, zh, c):
        return (y % Y * ZH + zh % ZH) * CORES + c % CORES

    return [(index(y, z, c), index(y + dy, z + dz, c + dc)) for y in range(Y) for z in range(ZH) for c in range(CORES)]


def train_shift(dx, dz):
    return [(x * ZL + z, (x + dx) % X * ZL + (z + dz) % ZL) for x in range(X) for z in range(ZL)]


def pick(a, at, axis):
    return lax.dynamic_index_in_dim(a, at, axis, keepdims=False)


def scores_kernel(mine_ref, a0, a1, a2, a3, b_own, b_other, *rest):
    *feats, keep, send, panel = rest
    mine = mine_ref[0]
    step = pl.program_id(0)

    @pl.when(step == 0)
    def _():
        for z in range(ZL):
            slot = (z + mine) % 2
            for k, a_ref in enumerate((a0, a1, a2, a3)):
                for s in range(2):
                    panel[slot, k, :, s * DEPTH : (s + 1) * DEPTH] = a_ref[z, s]
            for k in range(X):
                for s in range(2):
                    panel[slot, k, :, (s + 2) * DEPTH : (s + 3) * DEPTH] = (b_own, b_other)[z][k, s]

    def columns(blocks):
        total = None
        for s, block in enumerate(blocks):
            rows = panel[:, :, :, s * DEPTH : (s + 1) * DEPTH].reshape(2 * X * ROWS, DEPTH)
            term = lax.dot_general(rows, block[...], NT, preferred_element_type=F32)
            total = term if total is None else total + term
        total = total.reshape(2, X, ROWS, COLS)
        keep[...] = total[0]
        send[...] = total[1].astype(BF16)

    columns(feats)


def scores_part(mine, gathered, feats):
    whole = lambda a: pl.BlockSpec(a.shape, lambda i, _: (0,) * a.ndim)
    half = pl.BlockSpec((COLS, DEPTH), lambda i, _: (i, 0))
    out = lambda kind: jax.ShapeDtypeStruct((X, ROWS, TRAIN), kind)
    out_spec = pl.BlockSpec((X, ROWS, COLS), lambda i, _: (0, 0, i))
    return pl.pallas_call(
        scores_kernel,
        grid_spec=pltpu.PrefetchScalarGridSpec(
            num_scalar_prefetch=1,
            grid=(TRAIN // COLS,),
            in_specs=[whole(a) for a in gathered] + [half] * Y,
            out_specs=[out_spec, out_spec],
            scratch_shapes=[pltpu.VMEM((2, X, ROWS, Y * DEPTH), BF16)],
        ),
        out_shape=[out(F32), out(BF16)],
        cost_estimate=pl.CostEstimate(flops=4 * X * ROWS * Y * DEPTH * TRAIN, bytes_accessed=8 << 20, transcendentals=0),
    )(mine, *gathered, *feats)


def shards(precond, target_feats, train_feats):
    w, r = lax.axis_index("wide"), lax.axis_index("train")
    y, zh, c = w // (ZH * CORES), (w // CORES) % ZH, w % CORES
    x, zl = r // ZL, r % ZL

    def along(a, dx, dz):
        return lax.ppermute(a, "train", train_shift(dx, dz))

    part = lax.dot_general(target_feats, precond, NT, preferred_element_type=F32).astype(F16)
    got = lax.all_to_all(part.reshape(Y, X * ZL, ROWS, DEPTH), "train", 1, 1, tiled=True)
    feats_1 = lax.ppermute(train_feats, "wide", wide_shift(1, 0, 0))
    feats_3 = lax.ppermute(train_feats, "wide", wide_shift(-1, 0, 0))

    pieces = [jnp.sum(pick(got, (y + s) % Y, 0).astype(F32), 0).astype(BF16) for s in range(Y)]
    pieces = pieces[:1] + [lax.ppermute(pieces[s], "wide", wide_shift(s, 0, 0)) for s in range(1, Y)]
    a = jnp.stack(pieces[:2])
    b = jnp.stack(pieces[2:])
    a, b, own, feats_1, feats_3 = lax.optimization_barrier((a, b, train_feats, feats_1, feats_3))
    feats_2 = lax.ppermute(own, "wide", wide_shift(2, 0, 0))
    a = jnp.stack([a, along(a, 0, 1)])
    b = jnp.stack([b] + [along(b, k, 0) for k in range(1, X)])
    gathered = [a] + [along(a, k, 0) for k in range(1, X)] + [b, along(b, 0, 1)]

    feats = (train_feats, feats_1, feats_2, feats_3)
    keep, send = scores_part(((c + zl) % 2).reshape(1), gathered, feats)
    both = keep + lax.ppermute(send, "wide", wide_shift(0, 0, 1)).astype(F32)
    blocks = [pick(both, (x - zh - s + 2 * X) % X, 0) for s in range(ZH)]
    out = blocks[0]
    for s in range(1, ZH):
        out = out + lax.ppermute(blocks[s].astype(BF16), "wide", wide_shift(0, s, 0)).astype(F32)
    return out


def solution(mesh):
    in_specs = (P("wide", "train"), P(None, "train"), P("train", "wide"))
    out_specs = P("wide", "train")
    return jax.shard_map(shards, mesh=mesh, in_specs=in_specs, out_specs=out_specs, check_vma=False)
```

```python
import jax
import jax.numpy as jnp
from jax import lax
from jax.experimental import pallas as pl
from jax.experimental.pallas import tpu as pltpu
from jax.sharding import PartitionSpec as P

Y, ZH, CORES, X, ZL = 4, 4, 2, 4, 2
ROWS, DEPTH, TRAIN = 48, 512, 1024
COLS = 512
BF16, F16, F32 = jnp.bfloat16, jnp.float16, jnp.float32
NT = (((1,), (1,)), ((), ()))


def wide_index(y, zh, c):
    return (y % Y * ZH + zh % ZH) * CORES + c % CORES


def wide_shift(dy, dz, dc):
    return [
        (wide_index(y, z, c), wide_index(y + dy, z + dz, c + dc)) for y in range(Y) for z in range(ZH) for c in range(CORES)
    ]


def train_shift(dx, dz):
    return [(x * ZL + z, (x + dx) % X * ZL + (z + dz) % ZL) for x in range(X) for z in range(ZL)]


def pick(a, at, axis):
    return lax.dynamic_index_in_dim(a, at, axis, keepdims=False)


def scores_kernel(slots_ref, *refs):
    pieces, refs = refs[: X + 2], refs[X + 2 :]
    feats, (keep, send, panel, *staged, blocks, sems) = refs[: 2 * Y], refs[2 * Y :]
    loads = [pltpu.make_async_copy(p, at, sems.at[n]) for n, (p, at) in enumerate(zip(pieces, staged))]
    loads += [pltpu.make_async_copy(f, blocks.at[n], sems.at[len(pieces) + n]) for n, f in enumerate(feats)]
    for load in loads:
        load.start()
    for load in loads[: len(pieces)]:
        load.wait()
    for z in range(ZL):
        for k in range(X):
            slot = slots_ref[z * X + k]
            for s in range(Y):
                piece = staged[k][z, s] if s < 2 else staged[X + z][k, s - 2]
                panel[slot, :, s * DEPTH : (s + 1) * DEPTH] = piece
    for half in range(2):
        total = None
        for s in range(Y):
            n = half * Y + s
            loads[len(pieces) + n].wait()
            rows = panel[:, :, s * DEPTH : (s + 1) * DEPTH].reshape(2 * X * ROWS, DEPTH)
            term = lax.dot_general(rows, blocks[n], NT, preferred_element_type=F32)
            total = term if total is None else total + term
        total = total.reshape(2, X, ROWS, COLS)
        keep[:, :, half * COLS : (half + 1) * COLS] = total[0]
        send[:, :, half * COLS : (half + 1) * COLS] = total[1].astype(BF16)


def scores_part(slots, gathered, feats):
    anywhere, vmem = pl.BlockSpec(memory_space=pl.ANY), pl.BlockSpec(memory_space=pltpu.VMEM)
    out = lambda kind: jax.ShapeDtypeStruct((X, ROWS, TRAIN), kind)
    return pl.pallas_call(
        scores_kernel,
        in_specs=[pl.BlockSpec(memory_space=pltpu.SMEM)] + [anywhere] * (len(gathered) + len(feats)),
        out_specs=[vmem, vmem],
        out_shape=[out(F32), out(BF16)],
        scratch_shapes=[pltpu.VMEM((2 * X, ROWS, Y * DEPTH), BF16)]
        + [pltpu.VMEM(a.shape, BF16) for a in gathered]
        + [pltpu.VMEM((2 * Y, COLS, DEPTH), BF16), pltpu.SemaphoreType.DMA((len(gathered) + len(feats),))],
        cost_estimate=pl.CostEstimate(flops=4 * X * ROWS * Y * DEPTH * TRAIN, bytes_accessed=8 << 20, transcendentals=0),
        compiler_params=pltpu.CompilerParams(vmem_limit_bytes=56 << 20),
    )(slots, *gathered, *feats)


def shards(precond, target_feats, train_feats):
    w, r = lax.axis_index("wide"), lax.axis_index("train")
    y, zh, c = w // (ZH * CORES), (w // CORES) % ZH, w % CORES
    x, zl = r // ZL, r % ZL

    def along(a, dx, dz):
        return lax.ppermute(a, "train", train_shift(dx, dz))

    part = lax.dot_general(target_feats, precond, NT, preferred_element_type=F32).astype(F16)
    got = lax.all_to_all(part.reshape(Y, X * ZL, ROWS, DEPTH), "train", 1, 1, tiled=True)
    low, high = train_feats[: TRAIN // 2], train_feats[TRAIN // 2 :]
    low_1 = lax.ppermute(low, "wide", wide_shift(1, 0, 0))
    high_3 = lax.ppermute(high, "wide", wide_shift(-1, 0, 0))
    high_1 = lax.ppermute(high, "wide", wide_shift(1, 0, 0))
    low_3 = lax.ppermute(low, "wide", wide_shift(-1, 0, 0))
    got, low_1, high_3 = lax.optimization_barrier((got, low_1, high_3))

    pieces = [jnp.sum(pick(got, (y + s) % Y, 0).astype(F32), 0).astype(BF16) for s in range(Y)]
    pieces = pieces[:1] + [lax.ppermute(pieces[s], "wide", wide_shift(s, 0, 0)) for s in range(1, Y)]
    pieces[1], low_1, high_3, high_1, low_3 = lax.optimization_barrier((pieces[1], low_1, high_3, high_1, low_3))
    a = jnp.stack(pieces[:2])
    b = jnp.stack(pieces[2:])
    low_2 = lax.ppermute(low_1, "wide", wide_shift(1, 0, 0))
    high_2 = lax.ppermute(high_3, "wide", wide_shift(-1, 0, 0))
    a = jnp.stack([a, along(a, 0, 1)])
    b = jnp.stack([b] + [along(b, k, 0) for k in range(1, X)])
    gathered = [a] + [along(a, k, 0) for k in range(1, X)] + [b, along(b, 0, 1)]

    feats = (low, low_1, low_2, low_3, high, high_1, high_2, high_3)
    k = jnp.arange(X)[None, :]
    to_core = (jnp.arange(ZL)[:, None] + zl) % 2
    away = (x - k - zh + 2 * X) % ZH
    near = away % 2 == 1
    place = jnp.where(near, 2 + to_core, away // 2)
    owner = jnp.where(near, away // 2, to_core)
    slots = (place + X * (owner != c)).reshape(-1).astype(jnp.int32)
    keep, send = scores_part(slots, gathered, feats)
    both = keep + lax.ppermute(send, "wide", wide_shift(0, 0, 1)).astype(F32)
    to_near = [
        (wide_index(v, z, core), wide_index(v, z + (1 - 2 * core), core)) for v in range(Y) for z in range(ZH) for core in range(CORES)
    ]
    near = lax.ppermute(both[2:].astype(BF16), "wide", to_near)
    far = lax.ppermute(both[1].astype(BF16), "wide", wide_shift(0, 2, 0))
    other = lax.ppermute(pick(near, 1 - c, 0), "wide", wide_shift(0, 0, 1))
    return both[0] + pick(near, c, 0).astype(F32) + other.astype(F32) + far.astype(F32)


def solution(mesh):
    in_specs = (P("wide", "train"), P(None, "train"), P("train", "wide"))
    out_specs = P("wide", "train")
    return jax.shard_map(shards, mesh=mesh, in_specs=in_specs, out_specs=out_specs, check_vma=False)
```

```python
import jax
import jax.numpy as jnp
from jax import lax
from jax.experimental import pallas as pl
from jax.experimental.pallas import tpu as pltpu
from jax.sharding import PartitionSpec as P

Y, ZH, CORES, X, ZL = 4, 4, 2, 4, 2
ROWS, DEPTH, TRAIN = 48, 512, 1024
COLS = 512
BF16, F16, F32 = jnp.bfloat16, jnp.float16, jnp.float32
NT = (((1,), (1,)), ((), ()))


def wide_index(y, zh, c):
    return (y % Y * ZH + zh % ZH) * CORES + c % CORES


def wide_shift(dy, dz, dc):
    return [
        (wide_index(y, z, c), wide_index(y + dy, z + dz, c + dc)) for y in range(Y) for z in range(ZH) for c in range(CORES)
    ]


def train_shift(dx, dz):
    return [(x * ZL + z, (x + dx) % X * ZL + (z + dz) % ZL) for x in range(X) for z in range(ZL)]


def pick(a, at, axis):
    return lax.dynamic_index_in_dim(a, at, axis, keepdims=False)


def scores_kernel(slots_ref, *refs):
    pieces, refs = refs[: X + 2], refs[X + 2 :]
    feats, (keep, send, panel, *staged, blocks, sems) = refs[: 2 * Y], refs[2 * Y :]
    loads = [pltpu.make_async_copy(p, at, sems.at[n]) for n, (p, at) in enumerate(zip(pieces, staged))]
    loads += [pltpu.make_async_copy(f, blocks.at[n], sems.at[len(pieces) + n]) for n, f in enumerate(feats)]
    for load in loads:
        load.start()
    for load in loads[: len(pieces)]:
        load.wait()
    for z in range(ZL):
        for k in range(X):
            slot = slots_ref[z * X + k]
            for s in range(Y):
                piece = staged[X + z][k, s] if s < 2 else staged[k][z, s - 2]
                panel[slot, :, s * DEPTH : (s + 1) * DEPTH] = piece
    for half in range(2):
        total = None
        for s in range(Y):
            n = half * Y + s
            loads[len(pieces) + n].wait()
            rows = panel[:, :, s * DEPTH : (s + 1) * DEPTH].reshape(2 * X * ROWS, DEPTH)
            term = lax.dot_general(rows, blocks[n], NT, preferred_element_type=F32)
            total = term if total is None else total + term
        total = total.reshape(2, X, ROWS, COLS)
        keep[:, :, half * COLS : (half + 1) * COLS] = total[0]
        send[:, :, half * COLS : (half + 1) * COLS] = total[1].astype(BF16)


def scores_part(slots, gathered, feats):
    anywhere, vmem = pl.BlockSpec(memory_space=pl.ANY), pl.BlockSpec(memory_space=pltpu.VMEM)
    out = lambda kind: jax.ShapeDtypeStruct((X, ROWS, TRAIN), kind)
    return pl.pallas_call(
        scores_kernel,
        in_specs=[pl.BlockSpec(memory_space=pltpu.SMEM)] + [anywhere] * (len(gathered) + len(feats)),
        out_specs=[vmem, vmem],
        out_shape=[out(F32), out(BF16)],
        scratch_shapes=[pltpu.VMEM((2 * X, ROWS, Y * DEPTH), BF16)]
        + [pltpu.VMEM(a.shape, BF16) for a in gathered]
        + [pltpu.VMEM((2 * Y, COLS, DEPTH), BF16), pltpu.SemaphoreType.DMA((len(gathered) + len(feats),))],
        cost_estimate=pl.CostEstimate(flops=4 * X * ROWS * Y * DEPTH * TRAIN, bytes_accessed=8 << 20, transcendentals=0),
        compiler_params=pltpu.CompilerParams(vmem_limit_bytes=56 << 20),
    )(slots, *gathered, *feats)


def shards(precond, target_feats, train_feats):
    w, r = lax.axis_index("wide"), lax.axis_index("train")
    y, zh, c = w // (ZH * CORES), (w // CORES) % ZH, w % CORES
    x, zl = r // ZL, r % ZL

    def along(a, dx, dz):
        return lax.ppermute(a, "train", train_shift(dx, dz))

    part = lax.dot_general(target_feats, precond, NT, preferred_element_type=F32)
    part = lax.optimization_barrier(part).astype(F16)
    got = lax.all_to_all(part.reshape(Y, X * ZL, ROWS, DEPTH), "train", 1, 1, tiled=True)
    low, high = train_feats[: TRAIN // 2], train_feats[TRAIN // 2 :]
    low_1 = lax.ppermute(low, "wide", wide_shift(1, 0, 0))
    high_3 = lax.ppermute(high, "wide", wide_shift(-1, 0, 0))
    high_1 = lax.ppermute(high, "wide", wide_shift(1, 0, 0))
    low_3 = lax.ppermute(low, "wide", wide_shift(-1, 0, 0))
    got, low_1, high_3 = lax.optimization_barrier((got, low_1, high_3))

    pieces = [jnp.sum(pick(got, (y + s) % Y, 0).astype(F32), 0).astype(BF16) for s in range(Y)]
    pieces = pieces[:1] + [lax.ppermute(pieces[s], "wide", wide_shift(s, 0, 0)) for s in range(1, Y)]
    pieces[2], pieces[3], low_1, high_3, high_1, low_3 = lax.optimization_barrier((pieces[2], pieces[3], low_1, high_3, high_1, low_3))
    a = jnp.stack(pieces[2:])
    b = jnp.stack(pieces[:2])
    low_2 = lax.ppermute(low_1, "wide", wide_shift(1, 0, 0))
    high_2 = lax.ppermute(high_3, "wide", wide_shift(-1, 0, 0))
    a = jnp.stack([a, along(a, 0, 1)])
    b = jnp.stack([b] + [along(b, k, 0) for k in range(1, X)])
    gathered = [a] + [along(a, k, 0) for k in range(1, X)] + [b, along(b, 0, 1)]

    feats = (low, low_1, low_2, low_3, high, high_1, high_2, high_3)
    k = jnp.arange(X)[None, :]
    to_core = (jnp.arange(ZL)[:, None] + zl) % 2
    away = (x - k - zh + 2 * X) % ZH
    near = away % 2 == 1
    place = jnp.where(near, 2 + to_core, away // 2)
    owner = jnp.where(near, away // 2, to_core)
    slots = (place + X * (owner != c)).reshape(-1).astype(jnp.int32)
    keep, send = scores_part(slots, gathered, feats)
    both = keep + lax.ppermute(send, "wide", wide_shift(0, 0, 1)).astype(F32)
    to_near = [
        (wide_index(v, z, core), wide_index(v, z + (1 - 2 * core), core)) for v in range(Y) for z in range(ZH) for core in range(CORES)
    ]
    near = lax.ppermute(both[2:].astype(BF16), "wide", to_near)
    far = lax.ppermute(both[1].astype(BF16), "wide", wide_shift(0, 2, 0))
    other = lax.ppermute(pick(near, 1 - c, 0), "wide", wide_shift(0, 0, 1))
    return both[0] + pick(near, c, 0).astype(F32) + other.astype(F32) + far.astype(F32)


def solution(mesh):
    in_specs = (P("wide", "train"), P(None, "train"), P("train", "wide"))
    out_specs = P("wide", "train")
    return jax.shard_map(shards, mesh=mesh, in_specs=in_specs, out_specs=out_specs, check_vma=False)
```

```python
import jax
import jax.numpy as jnp
from jax import lax
from jax.experimental import pallas as pl
from jax.experimental.pallas import tpu as pltpu
from jax.sharding import PartitionSpec as P

Y, ZH, CORES, X, ZL = 4, 4, 2, 4, 2
ROWS, DEPTH, TRAIN = 48, 512, 1024
COLS = 512
BF16, F16, F32 = jnp.bfloat16, jnp.float16, jnp.float32
NT = (((1,), (1,)), ((), ()))


def wide_index(y, zh, c):
    return (y % Y * ZH + zh % ZH) * CORES + c % CORES


def wide_shift(dy, dz, dc):
    return [
        (wide_index(y, z, c), wide_index(y + dy, z + dz, c + dc)) for y in range(Y) for z in range(ZH) for c in range(CORES)
    ]


def train_shift(dx, dz):
    return [(x * ZL + z, (x + dx) % X * ZL + (z + dz) % ZL) for x in range(X) for z in range(ZL)]


def pick(a, at, axis):
    return lax.dynamic_index_in_dim(a, at, axis, keepdims=False)


def scores_kernel(slots_ref, *refs):
    pieces, refs = refs[: X + 2], refs[X + 2 :]
    feats, (keep, send, panel, *staged, blocks, sems) = refs[: 2 * Y], refs[2 * Y :]
    loads = [pltpu.make_async_copy(p, at, sems.at[n]) for n, (p, at) in enumerate(zip(pieces, staged))]
    loads += [pltpu.make_async_copy(f, blocks.at[n], sems.at[len(pieces) + n]) for n, f in enumerate(feats)]
    for load in loads:
        load.start()
    for load in loads[: len(pieces)]:
        load.wait()
    for z in range(ZL):
        for k in range(X):
            slot = slots_ref[z * X + k]
            for s in range(Y):
                piece = staged[X + z][k, s] if s < 2 else staged[k][z, s - 2]
                panel[slot, :, s * DEPTH : (s + 1) * DEPTH] = piece
    for half in range(2):
        total = None
        for s in range(Y):
            n = half * Y + s
            loads[len(pieces) + n].wait()
            rows = panel[:, :, s * DEPTH : (s + 1) * DEPTH].reshape(2 * X * ROWS, DEPTH)
            term = lax.dot_general(rows, blocks[n], NT, preferred_element_type=F32)
            total = term if total is None else total + term
        total = total.reshape(2, X, ROWS, COLS)
        keep[:, :, half * COLS : (half + 1) * COLS] = total[0]
        send[:, :, half * COLS : (half + 1) * COLS] = total[1].astype(BF16)


def scores_part(slots, gathered, feats):
    anywhere, vmem = pl.BlockSpec(memory_space=pl.ANY), pl.BlockSpec(memory_space=pltpu.VMEM)
    out = lambda kind: jax.ShapeDtypeStruct((X, ROWS, TRAIN), kind)
    return pl.pallas_call(
        scores_kernel,
        in_specs=[pl.BlockSpec(memory_space=pltpu.SMEM)] + [anywhere] * (len(gathered) + len(feats)),
        out_specs=[vmem, vmem],
        out_shape=[out(F32), out(BF16)],
        scratch_shapes=[pltpu.VMEM((2 * X, ROWS, Y * DEPTH), BF16)]
        + [pltpu.VMEM(a.shape, BF16) for a in gathered]
        + [pltpu.VMEM((2 * Y, COLS, DEPTH), BF16), pltpu.SemaphoreType.DMA((len(gathered) + len(feats),))],
        cost_estimate=pl.CostEstimate(flops=4 * X * ROWS * Y * DEPTH * TRAIN, bytes_accessed=8 << 20, transcendentals=0),
        compiler_params=pltpu.CompilerParams(vmem_limit_bytes=56 << 20),
    )(slots, *gathered, *feats)


def shards(precond, target_feats, train_feats):
    w, r = lax.axis_index("wide"), lax.axis_index("train")
    y, zh, c = w // (ZH * CORES), (w // CORES) % ZH, w % CORES
    x, zl = r // ZL, r % ZL

    def along(a, dx, dz):
        return lax.ppermute(a, "train", train_shift(dx, dz))

    part = lax.dot_general(target_feats, precond, NT, preferred_element_type=F32)
    part = lax.optimization_barrier(part).astype(F16)
    got = lax.all_to_all(part.reshape(Y, X * ZL, ROWS, DEPTH), "train", 1, 1, tiled=True)
    low, high = train_feats[: TRAIN // 2], train_feats[TRAIN // 2 :]
    low_1 = lax.ppermute(low, "wide", wide_shift(1, 0, 0))
    high_3 = lax.ppermute(high, "wide", wide_shift(-1, 0, 0))
    high_1 = lax.ppermute(high, "wide", wide_shift(1, 0, 0))
    low_3 = lax.ppermute(low, "wide", wide_shift(-1, 0, 0))
    got, low_1, high_3 = lax.optimization_barrier((got, low_1, high_3))

    pieces = [jnp.sum(pick(got, (y + s) % Y, 0).astype(F32), 0).astype(BF16) for s in range(Y)]
    pieces = pieces[:1] + [lax.ppermute(pieces[s], "wide", wide_shift(s, 0, 0)) for s in range(1, Y)]
    pieces[2], pieces[3], low_1, high_3, high_1, low_3 = lax.optimization_barrier((pieces[2], pieces[3], low_1, high_3, high_1, low_3))
    a = jnp.stack(pieces[2:])
    b = jnp.stack(pieces[:2])
    low_2 = lax.ppermute(low_1, "wide", wide_shift(1, 0, 0))
    high_2 = lax.ppermute(high_3, "wide", wide_shift(-1, 0, 0))
    a = jnp.stack([a, along(a, 0, 1)])
    b = jnp.stack([b] + [along(b, k, 0) for k in range(1, X)])
    gathered = [a] + [along(a, k, 0) for k in range(1, X)] + [b, along(b, 0, 1)]

    feats = (low, low_1, low_2, low_3, high, high_1, high_2, high_3)
    steps = ((0, 1, 2, 3), (0, 3, 2, 1))
    k = jnp.arange(X)[None, :]
    to_core = (jnp.arange(ZL)[:, None] + zl) % 2
    apart = ((x - k + X) % X) ^ zh
    slots = (apart + X * (to_core != c)).reshape(-1).astype(jnp.int32)
    keep, send = scores_part(slots, gathered, feats)
    both = keep + lax.ppermute(send, "wide", wide_shift(0, 0, 1)).astype(F32)

    def to(s):
        return [(wide_index(v, z, o), wide_index(v, z ^ steps[o][s], o)) for v in range(Y) for z in range(ZH) for o in range(CORES)]

    out = both[0]
    for s in range(1, ZH):
        block = both[2] if s == 2 else pick(both, jnp.where(c == 0, steps[0][s], steps[1][s]), 0)
        out = out + lax.ppermute(block.astype(BF16), "wide", to(s)).astype(F32)
    return out


def solution(mesh):
    in_specs = (P("wide", "train"), P(None, "train"), P("train", "wide"))
    out_specs = P("wide", "train")
    return jax.shard_map(shards, mesh=mesh, in_specs=in_specs, out_specs=out_specs, check_vma=False)
```
